32 devices in a mesh: ctx: 8 (over z, x), head: 4 (over y, core).
Axes of the slice: x: 2, y: 2, z: 4, core: 2. Of those that a mesh axis runs over, the one named last changes fastest.
Arguments:
- query_rows: bfloat16 [4096, 5120], P(('ctx', 'head')), may hold values from -6 to 6
- key_rows: bfloat16 [4096, 1024], P(('ctx', 'head')), may hold values from -6 to 6
- value_rows: bfloat16 [4096, 1024], P(('ctx', 'head')), may hold values from -6 to 6
- attn_output: bfloat16 [4096, 5120], P(('ctx', 'head')), may hold values from -3 to 3
- out_grad: bfloat16 [4096, 5120], P(('ctx', 'head')), may hold values from -24 to 24
- log_norm: float32 [40, 4096], P('head', 'ctx'), may hold values from 5 to 7
- prefix_keys: bfloat16 [128, 1024], P('ctx', 'head'), may hold values from -6 to 6
- prefix_values: bfloat16 [128, 1024], P('ctx', 'head'), may hold values from -6 to 6
- response_blocks: int32 [16], replicated, may hold values from 1 to 16, as said below
- prompt_members: int32 [1, 16], replicated, may hold values from 0 to 15, as said below
Outputs:
- query_grad: bfloat16 [4096, 5120], P('ctx', 'head')
- key_grad: bfloat16 [4096, 1024], P('ctx', 'head')
- value_grad: bfloat16 [4096, 1024], P('ctx', 'head')
- prefix_keygrads: bfloat16 [128, 1024], P('ctx', 'head')
- prefix_valuegrads: bfloat16 [128, 1024], P('ctx', 'head')
The draws below stay inside these ranges and needn't reach their ends.
Inputs may be any that keep to these rules, and one draw needn't show every extreme that they name: `response_blocks`: the lengths fill all 128 blocks of the row. Every index of ctx from 1 on begins inside a response that started on the index before it. `prompt_members`: every response, numbered 0 to 15 in order along the row, is listed exactly once.
All inputs are finite; a program needn't handle non-finite values.
Results may differ from the reference program's by a relative error of at most 0.008.
Values may be sent and summed in bfloat16 or wider, within the bound.
A program may use at most 64 MiB of HBM per device.

```python
import math
import jax
import jax.numpy as jnp
from jax import lax

QH = 40
KVH = 8
HD = 128
TOK_DEV = 512
BLK = 32
PL = 128
GROUP = 16
TOKENS = 4096
NBD = 16
NB = 128
NRESP = 16
NPROMPT = 1
N_CTX = 8


def draw_prompt_members(key, part):
    order = jax.random.permutation(key, NRESP)
    return order.reshape(NPROMPT, GROUP).astype(jnp.int32)


def draw_response_blocks(key, part):
    devices = NRESP // 2
    upper_key = jax.random.fold_in(key, 11)
    lower_key = jax.random.fold_in(key, 23)
    upper = jax.random.randint(upper_key, (devices,), 2, NBD).astype(jnp.int32)
    upper = upper.at[0].set(1)
    earlier = jnp.concatenate([jnp.ones((1,), jnp.int32), upper[:-1]])
    limit = jnp.maximum(jnp.minimum(earlier, upper - 1), 1).astype(jnp.int32)
    lower = jax.random.randint(lower_key, (devices,), 1, limit + 1).astype(jnp.int32)
    lower = lower.at[1].set(1)
    offsets = (jnp.arange(devices, dtype=jnp.int32) * NBD).astype(jnp.int32)
    inner = jnp.stack([offsets[1:] + lower[1:], offsets[1:] + upper[1:]], axis=1).reshape(-1)
    starts = jnp.concatenate([jnp.zeros((1,), jnp.int32), jnp.ones((1,), jnp.int32), inner.astype(jnp.int32)])
    ends = jnp.concatenate([starts[1:], jnp.full((1,), NB, jnp.int32)])
    return (ends - starts).astype(jnp.int32)


def block_scale(stream_key, shape, cuts, least, largest):
    factor_of, own = 1.0, jax.random.fold_in(stream_key, 6)
    for position, parts in cuts:
        steps = jnp.exp(jax.random.uniform(jax.random.fold_in(own, position), (parts,), jnp.float32, least / len(cuts), largest / len(cuts)))
        factor_of = factor_of * jnp.repeat(steps, shape[position] // parts).reshape([-1 if axis == position else 1 for axis in range(len(shape))])
    return factor_of


def normal_values(key, shape, spread, bound, split=(), kind=jnp.bfloat16):
    gain = block_scale(key, shape, split, -0.22, 0.18) if split else 1.0
    array = jax.random.normal(key, shape, jnp.float32) * spread * gain
    return jnp.minimum(jnp.maximum(array, -bound), bound).astype(kind)


def setup_inputs(seed: int = 0) -> dict:
    seeds = jax.random.split(jax.random.key(seed), 11)
    return {
        "query_rows": normal_values(seeds[0], (TOKENS, QH * HD), 1.0, 6.0, ((0, 32),)),
        "key_rows": normal_values(seeds[1], (TOKENS, KVH * HD), 1.0, 6.0, ((0, 32),)),
        "value_rows": normal_values(seeds[2], (TOKENS, KVH * HD), 1.0, 6.0, ((0, 32),)),
        "attn_output": normal_values(seeds[3], (TOKENS, QH * HD), 0.5, 3.0, ((0, 32),)),
        "out_grad": normal_values(seeds[4], (TOKENS, QH * HD), 4.0, 24.0, ((0, 32),)),
        "log_norm": jnp.clip(5.0 + 2.0 * jax.random.uniform(seeds[5], (QH, TOKENS), jnp.float32) ** block_scale(seeds[5], (QH, TOKENS), ((0, 4), (1, 8)), -0.2, 0.2), 5.0, 7.0),
        "prefix_keys": normal_values(seeds[6], (NPROMPT * PL, KVH * HD), 1.0, 6.0, ((0, 8), (1, 4))),
        "prefix_values": normal_values(seeds[7], (NPROMPT * PL, KVH * HD), 1.0, 6.0, ((0, 8), (1, 4))),
        "response_blocks": draw_response_blocks(jax.random.fold_in(seeds[10], 71), 0),
        "prompt_members": draw_prompt_members(jax.random.fold_in(seeds[10], 71), 0),
    }


def token_tables(response_blocks, prompt_members, first_block, count):
    lengths = response_blocks.astype(jnp.int32)
    starts = (jnp.cumsum(lengths) - lengths).astype(jnp.int32)
    responses = lengths.shape[0]
    group = prompt_members.shape[1]
    listed = prompt_members.reshape(-1).astype(jnp.int32)
    owner = (jnp.arange(listed.shape[0], dtype=jnp.int32) // group).astype(jnp.int32)
    numbers = jnp.arange(responses, dtype=jnp.int32)
    hits = listed[:, None] == numbers[None, :]
    prompt_of = lax.optimization_barrier(jnp.sum(jnp.where(hits, owner[:, None], 0), axis=0)).astype(jnp.int32)
    blocks = (first_block + jnp.arange(count, dtype=jnp.int32)).astype(jnp.int32)
    before = starts[None, :] <= blocks[:, None]
    first = lax.optimization_barrier(jnp.max(jnp.where(before, starts[None, :], 0), axis=1)).astype(jnp.int32)
    current = (lax.optimization_barrier(jnp.sum(before.astype(jnp.int32), axis=1)) - 1).astype(jnp.int32)
    chosen = numbers[None, :] == current[:, None]
    prompt_block = lax.optimization_barrier(jnp.sum(jnp.where(chosen, prompt_of[None, :], 0), axis=1)).astype(jnp.int32)
    return (jnp.repeat(first * BLK, BLK).astype(jnp.int32), jnp.repeat(prompt_block, BLK).astype(jnp.int32))

def tile_terms(queries, grads, norms, deltas, keys, values, allowed):
    rows = queries.shape[0]
    cols = keys.shape[0]
    heads = norms.shape[1]
    group = heads // (keys.shape[1] // HD)
    scale = 1.0 / math.sqrt(HD)

    def one_head(head, carry):
        query_acc, key_acc, value_acc = carry
        kv_head = head // group
        query_h = lax.dynamic_slice_in_dim(queries, head * HD, HD, 1)
        grad_h = lax.dynamic_slice_in_dim(grads, head * HD, HD, 1)
        key_h = lax.dynamic_slice_in_dim(keys, kv_head * HD, HD, 1)
        value_h = lax.dynamic_slice_in_dim(values, kv_head * HD, HD, 1)
        norm_h = lax.dynamic_slice_in_dim(norms, head, 1, 1)
        delta_h = lax.dynamic_slice_in_dim(deltas, head, 1, 1)
        logits = jnp.dot(query_h, key_h.T, preferred_element_type=jnp.float32)
        weights = jnp.where(allowed, jnp.exp(logits * scale - norm_h), 0.0)
        weights_b = weights.astype(jnp.bfloat16)
        value_term = jnp.dot(weights_b.T, grad_h, preferred_element_type=jnp.float32)
        dweights = jnp.dot(grad_h, value_h.T, preferred_element_type=jnp.float32)
        dlogits = (weights * (dweights - delta_h)).astype(jnp.bfloat16)
        query_term = jnp.dot(dlogits, key_h, preferred_element_type=jnp.float32)
        key_term = jnp.dot(dlogits.T, query_h, preferred_element_type=jnp.float32)
        query_acc = lax.dynamic_update_slice_in_dim(query_acc, query_term, head * HD, 1)
        old_key = lax.dynamic_slice_in_dim(key_acc, kv_head * HD, HD, 1)
        key_acc = lax.dynamic_update_slice_in_dim(key_acc, old_key + key_term, kv_head * HD, 1)
        old_value = lax.dynamic_slice_in_dim(value_acc, kv_head * HD, HD, 1)
        value_acc = lax.dynamic_update_slice_in_dim(value_acc, old_value + value_term, kv_head * HD, 1)
        return (query_acc, key_acc, value_acc)
    start = (jnp.zeros((rows, queries.shape[1]), jnp.float32), jnp.zeros((cols, keys.shape[1]), jnp.float32), jnp.zeros((cols, keys.shape[1]), jnp.float32))
    return lax.fori_loop(0, heads, one_head, start)

def add_rows(total, term, offset):
    old = lax.dynamic_slice_in_dim(total, offset, term.shape[0], 0)
    return lax.dynamic_update_slice_in_dim(total, old + term, offset, 0)

def reference(query_rows, key_rows, value_rows, attn_output, out_grad, log_norm, prefix_keys, prefix_values, response_blocks, prompt_members):
    kv_width = key_rows.shape[1]
    scale = 1.0 / math.sqrt(HD)
    positions = jnp.arange(TOK_DEV, dtype=jnp.int32)

    def block_step(carry, index):
        key_acc, value_acc, pkey_acc, pvalue_acc = carry
        base = (index * TOK_DEV).astype(jnp.int32)
        prior = (jnp.maximum(index - 1, 0) * TOK_DEV).astype(jnp.int32)
        queries = lax.dynamic_slice_in_dim(query_rows, base, TOK_DEV, 0)
        grads = lax.dynamic_slice_in_dim(out_grad, base, TOK_DEV, 0)
        outputs = lax.dynamic_slice_in_dim(attn_output, base, TOK_DEV, 0)
        norms = lax.dynamic_slice_in_dim(log_norm, base, TOK_DEV, 1).T
        deltas = jnp.einsum('thd,thd->th', grads.reshape(TOK_DEV, QH, HD).astype(jnp.float32), outputs.reshape(TOK_DEV, QH, HD).astype(jnp.float32))
        keys_here = lax.dynamic_slice_in_dim(key_rows, base, TOK_DEV, 0)
        values_here = lax.dynamic_slice_in_dim(value_rows, base, TOK_DEV, 0)
        keys_prior = lax.dynamic_slice_in_dim(key_rows, prior, TOK_DEV, 0)
        values_prior = lax.dynamic_slice_in_dim(value_rows, prior, TOK_DEV, 0)
        starts, prompts = token_tables(response_blocks, prompt_members, index * NBD, NBD)
        local_start = starts - base
        allowed_here = (positions[None, :] >= local_start[:, None]) & (positions[None, :] <= positions[:, None])
        allowed_prior = positions[None, :] - TOK_DEV >= local_start[:, None]
        query_one, key_one, value_one = tile_terms(queries, grads, norms, deltas, keys_here, values_here, allowed_here)
        query_two, key_two, value_two = tile_terms(queries, grads, norms, deltas, keys_prior, values_prior, allowed_prior)
        query_total = query_one + query_two

        def prompt_step(number, state):

            def compute(inner):
                total, pkeys, pvalues = inner
                keys_p = lax.dynamic_slice_in_dim(prefix_keys, number * PL, PL, 0)
                values_p = lax.dynamic_slice_in_dim(prefix_values, number * PL, PL, 0)
                allowed = jnp.broadcast_to((prompts == number)[:, None], (TOK_DEV, PL))
                query_p, key_p, value_p = tile_terms(queries, grads, norms, deltas, keys_p, values_p, allowed)
                return (total + query_p, add_rows(pkeys, key_p, number * PL), add_rows(pvalues, value_p, number * PL))
            return lax.cond(jnp.any(prompts == number), compute, lambda inner: inner, state)
        query_total, pkey_acc, pvalue_acc = lax.fori_loop(0, NPROMPT, prompt_step, (query_total, pkey_acc, pvalue_acc))
        key_acc = add_rows(add_rows(key_acc, key_one, base), key_two, prior)
        value_acc = add_rows(add_rows(value_acc, value_one, base), value_two, prior)
        return ((key_acc, value_acc, pkey_acc, pvalue_acc), (query_total * scale).astype(jnp.bfloat16))
    init = (jnp.zeros((TOKENS, kv_width), jnp.float32), jnp.zeros((TOKENS, kv_width), jnp.float32), jnp.zeros((NPROMPT * PL, kv_width), jnp.float32), jnp.zeros((NPROMPT * PL, kv_width), jnp.float32))
    carry, query_blocks = lax.scan(block_step, init, jnp.arange(N_CTX, dtype=jnp.int32))
    key_acc, value_acc, pkey_acc, pvalue_acc = carry
    query_grad = query_blocks.reshape(TOKENS, QH * HD)
    return (query_grad, (key_acc * scale).astype(jnp.bfloat16), value_acc.astype(jnp.bfloat16), (pkey_acc * scale).astype(jnp.bfloat16), pvalue_acc.astype(jnp.bfloat16))
```

```python
import functools
import math

import jax
import jax.numpy as jnp
from jax import lax
from jax.experimental import pallas as pl
from jax.experimental.pallas import tpu as pltpu
from jax.sharding import PartitionSpec as P

HD = 128
BLK = 32
PL = 128
AHEAD = 3
NEG = -1e30
LOG2E = math.log2(math.e)
F32 = jnp.float32
BF16 = jnp.bfloat16
MESH = pl.DeviceIdType.MESH
NT = (((1,), (1,)), ((), ()))


def kernel(
    q_hbm, k_hbm, v_hbm, o_hbm, g_hbm, norm_ref, pk_ref, pv_ref, blocks_ref, members_ref,
    dq_hbm, dk_ref, dv_ref, dpk_ref, dpv_ref,
    q_all, g_all, k_all, v_all, kp, vp, pk_all, pv_all, kt, g_vm, o_vm,
    dl_send, dl_recv, bias, prompt_of, starts_s,
    dq_acc, dq_out, dk_acc, dv_acc, dkp, dvp, bk_send, bk_recv, pacc, precv,
    q_snd, g_snd, q_rcv, g_rcv, kv_snd, kv_rcv, fw_snd, fw_rcv, pg_snd, pg_rcv,
    pr_snd, pr_rcv, bk_snd_sem, bk_rcv_sem, dl_snd_sem, dl_rcv_sem, loc, dq_sem,
    *, n_ctx, n_head, nprompt, own, kvl,
):
    me = lax.axis_index("head")
    cx = lax.axis_index("ctx")
    rows = q_hbm.shape[0]
    tokens = rows * n_head
    width = own * HD
    kvw = kvl * HD
    grp = own // kvl
    scale = 1.0 / math.sqrt(HD)
    ptot = nprompt * PL
    part = ptot // n_ctx
    nresp = blocks_ref.shape[0]
    members = members_ref.shape[1]
    slot = dl_send.shape[1]
    mine = pl.ds(pl.multiple_of(me * rows, rows), rows)

    def from_rows(s):
        return pl.ds(pl.multiple_of(s * rows, rows), rows)

    def head_cols(dst, h):
        return pl.ds(pl.multiple_of(dst * width + h * HD, HD), HD)

    def kv_cols(dst):
        return pl.ds(pl.multiple_of(dst * kvw, HD), kvw)

    def part_rows(c):
        return pl.ds(pl.multiple_of(c * part, part), part)

    def remote(src, dst, snd, rcv, **to):
        return pltpu.make_async_remote_copy(
            src_ref=src, dst_ref=dst, send_sem=snd, recv_sem=rcv, device_id=to,
            device_id_type=MESH,
        )

    def arrived(ref, sem):
        pltpu.make_async_copy(ref, ref, sem).wait()

    def peer(off):
        return lax.rem(me + off, n_head)

    def q_copy(h, off):
        dst = peer(off)
        return (
            remote(q_hbm.at[:, head_cols(dst, h)], q_all.at[h, mine], q_snd.at[h, dst],
                   q_rcv.at[h, me], head=dst),
            remote(g_hbm.at[:, head_cols(dst, h)], g_all.at[h, mine], g_snd.at[h, dst],
                   g_rcv.at[h, me], head=dst),
        )

    def q_local(h):
        return (
            pltpu.make_async_copy(q_hbm.at[:, head_cols(me, h)], q_all.at[h, mine], q_rcv.at[h, me]),
            pltpu.make_async_copy(g_hbm.at[:, head_cols(me, h)], g_all.at[h, mine], g_rcv.at[h, me]),
        )

    def send_head(h):
        for off in (2, 1, 3):
            for c in q_copy(h, off):
                c.start()
        for c in q_local(h):
            c.start()

    def kv_copy(off):
        dst = peer(off)
        return (
            remote(k_hbm.at[:, kv_cols(dst)], k_all.at[mine], kv_snd.at[0, dst], kv_rcv.at[0, me], head=dst),
            remote(v_hbm.at[:, kv_cols(dst)], v_all.at[mine], kv_snd.at[1, dst], kv_rcv.at[1, me], head=dst),
        )

    def forward(s):
        r = from_rows(s)
        return (
            remote(k_all.at[r], kp.at[r], fw_snd.at[0, s], fw_rcv.at[0, s], ctx=cx + 1),
            remote(v_all.at[r], vp.at[r], fw_snd.at[1, s], fw_rcv.at[1, s], ctx=cx + 1),
        )

    def prefix_copy(off):
        dst = lax.rem(cx + off, n_ctx)
        r = part_rows(cx)
        return (
            remote(pk_ref, pk_all.at[r], pg_snd.at[0, dst], pg_rcv.at[0, cx], ctx=dst),
            remote(pv_ref, pv_all.at[r], pg_snd.at[1, dst], pg_rcv.at[1, cx], ctx=dst),
        )

    def back(kv):
        return remote(bk_send.at[kv], bk_recv.at[kv], bk_snd_sem.at[kv], bk_rcv_sem.at[kv], ctx=cx - 1)

    def reduce_copy(kv, off):
        dst = lax.rem(cx + off, n_ctx)
        return remote(pacc.at[kv, dst], precv.at[kv, cx], pr_snd.at[kv, dst], pr_rcv.at[kv, cx], ctx=dst)

    def delta_copy(off):
        dst = peer(off)
        return remote(dl_send.at[dst], dl_recv.at[me], dl_snd_sem.at[dst], dl_rcv_sem.at[me], head=dst)

    def over_ctx(body):
        def step(off, carry):
            body(off)
            return carry
        lax.fori_loop(1, n_ctx, step, 0)

    barrier = pltpu.get_barrier_semaphore()
    for off in range(1, n_head):
        pl.semaphore_signal(barrier, inc=1, device_id={"head": peer(off)}, device_id_type=MESH)
    over_ctx(lambda off: pl.semaphore_signal(
        barrier, inc=1, device_id={"ctx": lax.rem(cx + off, n_ctx)}, device_id_type=MESH))

    get_g = pltpu.make_async_copy(g_hbm, g_vm, loc.at[0])
    get_o = pltpu.make_async_copy(o_hbm, o_vm, loc.at[1])
    get_g.start()
    get_o.start()
    own_kv = (
        pltpu.make_async_copy(k_hbm.at[:, kv_cols(me)], k_all.at[mine], loc.at[2]),
        pltpu.make_async_copy(v_hbm.at[:, kv_cols(me)], v_all.at[mine], loc.at[3]),
    )
    for c in own_kv:
        c.start()
    pl.semaphore_wait(barrier, n_head - 1 + n_ctx - 1)

    for off in (2, 1, 3):
        for c in kv_copy(off):
            c.start()
    for h in range(AHEAD):
        send_head(h)
    for c in own_kv:
        c.wait()

    @pl.when(cx < n_ctx - 1)
    def _():
        for c in forward(me):
            c.start()

    def prefix_start(off):
        for c in prefix_copy(off):
            c.start()
    over_ctx(prefix_start)
    pk_all[part_rows(cx)] = pk_ref[...]
    pv_all[part_rows(cx)] = pv_ref[...]

    get_g.wait()
    get_o.wait()
    lane = lax.broadcasted_iota(jnp.int32, (rows, HD), 1)
    cols = jnp.zeros((rows, HD), F32)
    for d in range(n_head):
        for j in range(own):
            c = (d * own + j) * HD
            term = g_vm[:, c:c + HD].astype(F32) * o_vm[:, c:c + HD].astype(F32)
            total = jnp.sum(term, axis=1, keepdims=True)
            cols = jnp.where(lane == d * slot + j, total, cols)
    flipped = cols.T
    for d in range(n_head):
        dl_send[d] = flipped[d * slot:(d + 1) * slot]
    dl_recv[me] = dl_send[me]
    for off in (2, 1, 3):
        delta_copy(off).start()

    for off in (1, 3, 2):
        s = peer(off)
        arrived(k_all.at[from_rows(s)], kv_rcv.at[0, s])
        arrived(v_all.at[from_rows(s)], kv_rcv.at[1, s])

        @pl.when(cx < n_ctx - 1)
        def _():
            for c in forward(s):
                c.start()

    def scan(r, total):
        starts_s[r] = total
        return total + blocks_ref[r]
    lax.fori_loop(0, nresp, scan, jnp.int32(0))
    block = cx * (tokens // BLK) + lax.broadcasted_iota(jnp.int32, (1, tokens), 1) // BLK

    def place(i, carry):
        first, owner = carry
        p = i // members
        r = members_ref[p, lax.rem(i, members)]
        low = starts_s[r]
        inside = (block >= low) & (block < low + blocks_ref[r])
        return (jnp.where(inside, low * BLK, first), jnp.where(inside, p, owner))

    zero = jnp.zeros((1, tokens), jnp.int32)
    first, owner = lax.fori_loop(0, nprompt * members, place, (zero, zero))
    prompt_of[...] = owner
    first = first - cx * tokens
    key_at = lax.broadcasted_iota(jnp.int32, (tokens, tokens), 0)
    tok_at = lax.broadcasted_iota(jnp.int32, (tokens, tokens), 1)
    bias[0:tokens] = jnp.where(key_at - tokens >= first, 0.0, NEG)
    bias[tokens:2 * tokens] = jnp.where((key_at >= first) & (key_at <= tok_at), 0.0, NEG)

    def prefix_wait(off):
        s = lax.rem(cx + off, n_ctx)
        arrived(pk_all.at[part_rows(s)], pg_rcv.at[0, s])
        arrived(pv_all.at[part_rows(s)], pg_rcv.at[1, s])
    over_ctx(prefix_wait)
    for off in (1, 3, 2):
        s = peer(off)
        arrived(dl_recv.at[s], dl_rcv_sem.at[s])

    @pl.when(cx > 0)
    def _():
        for s in range(n_head):
            arrived(kp.at[s * rows:(s + 1) * rows], fw_rcv.at[0, s])
            arrived(vp.at[s * rows:(s + 1) * rows], fw_rcv.at[1, s])

    dk_acc[...] = jnp.zeros_like(dk_acc)
    dv_acc[...] = jnp.zeros_like(dv_acc)
    pacc[...] = jnp.zeros_like(pacc)

    @pl.when(cx > 0)
    def _():
        dkp[...] = jnp.zeros_like(dkp)
        dvp[...] = jnp.zeros_like(dvp)

    for kv in range(kvl):
        kc = slice(kv * HD, (kv + 1) * HD)
        kt[:, 0:ptot] = pk_all[:, kc].T
        kt[:, ptot + tokens:ptot + 2 * tokens] = k_all[:, kc].T

        @pl.when(cx > 0)
        def _():
            kt[:, ptot:ptot + tokens] = kp[:, kc].T

        def terms(keys, values, keys_t, qs, gs, norm, delta, mask):
            logits = lax.dot_general(keys, qs, NT, preferred_element_type=F32)
            weights = jnp.exp2(logits * (scale * LOG2E) + (mask - norm))
            weights_b = weights.astype(BF16)
            dv = jnp.dot(weights_b, gs, preferred_element_type=F32)
            dw = lax.dot_general(values, gs, NT, preferred_element_type=F32)
            dl = (weights * (dw - delta)).astype(BF16)
            dk = jnp.dot(dl, qs, preferred_element_type=F32)
            dq = jnp.dot(keys_t, dl, preferred_element_type=F32)
            return dq, dk, dv

        def one_head(i, carry):
            h = kv * grp + i

            @pl.when(h + AHEAD < own)
            def _():
                send_head(h + AHEAD)

            for off in (0, 1, 3, 2):
                s = peer(off)
                arrived(q_all.at[h, from_rows(s)], q_rcv.at[h, s])
                arrived(g_all.at[h, from_rows(s)], g_rcv.at[h, s])
            norm = norm_ref[pl.ds(h, 1), :] * LOG2E
            delta = jnp.concatenate(
                [dl_recv[s, pl.ds(h, 1), :] for s in range(n_head)], axis=1)
            qs = q_all[h]
            gs = g_all[h]

            def prompt(p, carry):
                r = pl.ds(pl.multiple_of(p * PL, PL), PL)
                if nprompt == 1:
                    mask = 0.0
                else:
                    mask = jnp.where(prompt_of[...] == p, 0.0, NEG)
                dq, dk, dv = terms(pk_all[r, kc], pv_all[r, kc], kt[:, r], qs, gs, norm, delta, mask)
                c = pl.ds(p * (PL // part), PL // part)
                pacc[kv, c, 0] += dk.reshape(PL // part, part, HD)
                pacc[kv, c, 1] += dv.reshape(PL // part, part, HD)
                if nprompt == 1:
                    dq_acc[...] = dq
                else:
                    dq_acc[...] += dq
                return carry

            if nprompt == 1:
                prompt(0, 0)
            else:
                dq_acc[...] = jnp.zeros_like(dq_acc)
                lax.fori_loop(0, nprompt, prompt, 0)

            kb = tokens // 2
            for b in range(2):
                a, e = b * kb, (b + 1) * kb
                t = slice(a, tokens)
                dq, dk, dv = terms(
                    k_all[a:e, kc], v_all[a:e, kc], kt[:, ptot + tokens + a:ptot + tokens + e],
                    qs[t], gs[t], norm[:, t], delta[:, t], bias[tokens + a:tokens + e, t])
                dk_acc[kv, a:e] += dk
                dv_acc[kv, a:e] += dv
                dq_acc[:, t] += dq

            @pl.when(cx > 0)
            def _():
                for b in range(2):
                    a, e = b * kb, (b + 1) * kb
                    dq, dk, dv = terms(
                        kp[a:e, kc], vp[a:e, kc], kt[:, ptot + a:ptot + e],
                        qs, gs, norm, delta, bias[a:e])
                    dkp[kv, a:e] += dk
                    dvp[kv, a:e] += dv
                    dq_acc[...] += dq

            dq_out[h] = (dq_acc[...] * scale).T.astype(BF16)
            pltpu.make_async_copy(
                dq_out.at[h], dq_hbm.at[:, pl.ds(pl.multiple_of(h * HD, HD), HD)], dq_sem.at[h]
            ).start()
            return carry

        lax.fori_loop(0, grp, one_head, 0)

        @pl.when(cx > 0)
        def _():
            bk_send[kv, 0] = dkp[kv].astype(BF16)
            bk_send[kv, 1] = dvp[kv].astype(BF16)
            back(kv).start()

        over_ctx(lambda off: reduce_copy(kv, off).start())
        precv[kv, cx] = pacc[kv, cx]

    for kv in range(kvl):
        kc = slice(kv * HD, (kv + 1) * HD)

        def sum_wait(off):
            s = lax.rem(cx + off, n_ctx)
            arrived(precv.at[kv, s], pr_rcv.at[kv, s])
        over_ctx(sum_wait)
        total = lax.fori_loop(0, n_ctx, lambda s, t: t + precv[kv, s], jnp.zeros((2, part, HD), F32))
        dpk_ref[:, kc] = (total[0] * scale).astype(BF16)
        dpv_ref[:, kc] = total[1].astype(BF16)

        @pl.when(cx < n_ctx - 1)
        def _():
            arrived(bk_recv.at[kv], bk_rcv_sem.at[kv])
            dk_ref[:, kc] = ((dk_acc[kv] + bk_recv[kv, 0].astype(F32)) * scale).astype(BF16)
            dv_ref[:, kc] = (dv_acc[kv] + bk_recv[kv, 1].astype(F32)).astype(BF16)

        @pl.when(cx == n_ctx - 1)
        def _():
            dk_ref[:, kc] = (dk_acc[kv] * scale).astype(BF16)
            dv_ref[:, kc] = dv_acc[kv].astype(BF16)

    def finish(h, carry):
        pltpu.make_async_copy(
            dq_out.at[h], dq_hbm.at[:, pl.ds(pl.multiple_of(h * HD, HD), HD)], dq_sem.at[h]
        ).wait()
        for off in (2, 1, 3):
            for c in q_copy(h, off):
                c.wait_send()
        return carry
    lax.fori_loop(0, own, finish, 0)
    for off in (2, 1, 3):
        for c in kv_copy(off):
            c.wait_send()
        delta_copy(off).wait_send()

    @pl.when(cx < n_ctx - 1)
    def _():
        for s in range(n_head):
            for c in forward(s):
                c.wait_send()

    @pl.when(cx > 0)
    def _():
        for kv in range(kvl):
            back(kv).wait_send()

    def sent(off):
        for c in prefix_copy(off):
            c.wait_send()
        for kv in range(kvl):
            reduce_copy(kv, off).wait_send()
    over_ctx(sent)


def shards(n_ctx, n_head, *arrays):
    query_rows, key_rows, _, _, _, log_norm, prefix_keys, _, blocks, members = arrays
    rows, total_width = query_rows.shape
    own = log_norm.shape[0]
    kvw = prefix_keys.shape[1]
    kvl = kvw // HD
    tokens = rows * n_head
    nprompt = members.shape[0]
    ptot = nprompt * PL
    part = prefix_keys.shape[0]
    slot = -(-own // 8) * 8
    hbm = pl.BlockSpec(memory_space=pl.ANY)
    vmem = pl.BlockSpec(memory_space=pltpu.VMEM)
    smem = pl.BlockSpec(memory_space=pltpu.SMEM)
    dma = pltpu.SemaphoreType.DMA
    return pl.pallas_call(
        functools.partial(
            kernel, n_ctx=n_ctx, n_head=n_head, nprompt=nprompt, own=own, kvl=kvl),
        out_shape=(
            jax.ShapeDtypeStruct((tokens, own * HD), BF16),
            jax.ShapeDtypeStruct((tokens, kvw), BF16),
            jax.ShapeDtypeStruct((tokens, kvw), BF16),
            jax.ShapeDtypeStruct((part, kvw), BF16),
            jax.ShapeDtypeStruct((part, kvw), BF16),
        ),
        in_specs=[hbm] * 5 + [vmem] * 3 + [smem] * 2,
        out_specs=(hbm, vmem, vmem, vmem, vmem),
        scratch_shapes=[
            pltpu.VMEM((own, tokens, HD), BF16),
            pltpu.VMEM((own, tokens, HD), BF16),
            pltpu.VMEM((tokens, kvw), BF16),
            pltpu.VMEM((tokens, kvw), BF16),
            pltpu.VMEM((tokens, kvw), BF16),
            pltpu.VMEM((tokens, kvw), BF16),
            pltpu.VMEM((ptot, kvw), BF16),
            pltpu.VMEM((ptot, kvw), BF16),
            pltpu.VMEM((HD, ptot + 2 * tokens), BF16),
            pltpu.VMEM((rows, total_width), BF16),
            pltpu.VMEM((rows, total_width), BF16),
            pltpu.VMEM((n_head, slot, rows), F32),
            pltpu.VMEM((n_head, slot, rows), F32),
            pltpu.VMEM((2 * tokens, tokens), F32),
            pltpu.VMEM((1, tokens), jnp.int32),
            pltpu.SMEM(blocks.shape, jnp.int32),
            pltpu.VMEM((HD, tokens), F32),
            pltpu.VMEM((own, tokens, HD), BF16),
            pltpu.VMEM((kvl, tokens, HD), F32),
            pltpu.VMEM((kvl, tokens, HD), F32),
            pltpu.VMEM((kvl, tokens, HD), F32),
            pltpu.VMEM((kvl, tokens, HD), F32),
            pltpu.VMEM((kvl, 2, tokens, HD), BF16),
            pltpu.VMEM((kvl, 2, tokens, HD), BF16),
            pltpu.VMEM((kvl, n_ctx, 2, part, HD), F32),
            pltpu.VMEM((kvl, n_ctx, 2, part, HD), F32),
            dma((own, n_head)), dma((own, n_head)), dma((own, n_head)), dma((own, n_head)),
            dma((2, n_head)), dma((2, n_head)), dma((2, n_head)), dma((2, n_head)),
            dma((2, n_ctx)), dma((2, n_ctx)),
            dma((kvl, n_ctx)), dma((kvl, n_ctx)),
            dma((kvl,)), dma((kvl,)),
            dma((n_head,)), dma((n_head,)),
            dma((4,)), dma((own,)),
        ],
        compiler_params=pltpu.CompilerParams(
            collective_id=0, has_side_effects=True, vmem_limit_bytes=48 * 1024 * 1024),
    )(*arrays)


def solution(mesh):
    placed = (
        P(("ctx", "head"), None),
        P(("ctx", "head"), None),
        P(("ctx", "head"), None),
        P(("ctx", "head"), None),
        P(("ctx", "head"), None),
        P("head", "ctx"),
        P("ctx", "head"),
        P("ctx", "head"),
        P(),
        P(),
    )
    return jax.shard_map(
        functools.partial(shards, mesh.shape["ctx"], mesh.shape["head"]),
        mesh=mesh,
        in_specs=placed,
        out_specs=(
            P("ctx", "head"),
            P("ctx", "head"),
            P("ctx", "head"),
            P("ctx", "head"),
            P("ctx", "head"),
        ),
        check_vma=False,
    )
```

```python
import functools
import math

import jax
import jax.numpy as jnp
from jax import lax
from jax.experimental import pallas as pl
from jax.experimental.pallas import tpu as pltpu
from jax.sharding import PartitionSpec as P

HD = 128
BLK = 32
PL = 128
EARLY = 1
AHEAD = 3
LAG = 2
PIECES = 4
VMEM_BYTES = 60 * 1024 * 1024
NEG = -1e30
LOG2E = math.log2(math.e)
F32 = jnp.float32
BF16 = jnp.bfloat16
MESH = pl.DeviceIdType.MESH
NT = (((1,), (1,)), ((), ()))


def kernel(
    q_hbm, k_hbm, v_hbm, o_hbm, g_hbm, norm_hbm, pk_ref, pv_ref, blocks_hbm, members_hbm,
    dq_hbm, dk_ref, dv_ref, dpk_ref, dpv_ref,
    q_all, g_all, k_all, v_all, kp, vp, pk_all, pv_all, kt, g_vm, o_vm,
    norm_ref, blocks_ref, members_ref, dl_send, dl_recv, bias, prompt_of, starts_s,
    dq_acc, dq_out, dk_acc, dv_acc, dkp, dvp, bk_send, bk_recv, pacc, psend, precv,
    q_snd, g_snd, q_rcv, g_rcv, kv_snd, kv_rcv, fw_snd, fw_rcv, pg_snd, pg_rcv,
    pr_snd, pr_rcv, bk_snd_sem, bk_rcv_sem, dl_snd_sem, dl_rcv_sem, loc, dq_sem,
    *, n_ctx, n_head, nprompt, own, kvl,
):
    me = lax.axis_index("head")
    cx = lax.axis_index("ctx")
    rows = q_hbm.shape[0]
    tokens = rows * n_head
    width = own * HD
    kvw = kvl * HD
    grp = own // kvl
    scale = 1.0 / math.sqrt(HD)
    ptot = nprompt * PL
    part = ptot // n_ctx
    nresp = blocks_ref.shape[0]
    members = members_ref.shape[1]
    slot = dl_send.shape[1]
    mine = pl.ds(pl.multiple_of(me * rows, rows), rows)

    def from_rows(s):
        return pl.ds(pl.multiple_of(s * rows, rows), rows)

    def head_cols(dst, h):
        return pl.ds(pl.multiple_of(dst * width + h * HD, HD), HD)

    def kv_cols(dst):
        return pl.ds(pl.multiple_of(dst * kvw, HD), kvw)

    def part_rows(c):
        return pl.ds(pl.multiple_of(c * part, part), part)

    def remote(src, dst, snd, rcv, **to):
        return pltpu.make_async_remote_copy(
            src_ref=src, dst_ref=dst, send_sem=snd, recv_sem=rcv, device_id=to,
            device_id_type=MESH,
        )

    def arrived(ref, sem):
        pltpu.make_async_copy(ref, ref, sem).wait()

    def peer(off):
        return lax.rem(me + off, n_head)

    def q_copy(h, off):
        dst = peer(off)
        return (
            remote(q_hbm.at[:, head_cols(dst, h)], q_all.at[h, mine], q_snd.at[h, dst],
                   q_rcv.at[h, me], head=dst),
            remote(g_hbm.at[:, head_cols(dst, h)], g_all.at[h, mine], g_snd.at[h, dst],
                   g_rcv.at[h, me], head=dst),
        )

    def q_local(h):
        return (
            pltpu.make_async_copy(q_hbm.at[:, head_cols(me, h)], q_all.at[h, mine], q_rcv.at[h, me]),
            pltpu.make_async_copy(g_hbm.at[:, head_cols(me, h)], g_all.at[h, mine], g_rcv.at[h, me]),
        )

    def send_head(h):
        for off in (2, 1, 3):
            for c in q_copy(h, off):
                c.start()
        for c in q_local(h):
            c.start()

    def kv_copy(off):
        dst = peer(off)
        return (
            remote(k_hbm.at[:, kv_cols(dst)], k_all.at[mine], kv_snd.at[0, dst], kv_rcv.at[0, me], head=dst),
            remote(v_hbm.at[:, kv_cols(dst)], v_all.at[mine], kv_snd.at[1, dst], kv_rcv.at[1, me], head=dst),
        )

    def forward(s):
        r = from_rows(s)
        return (
            remote(k_all.at[r], kp.at[r], fw_snd.at[0, s], fw_rcv.at[0, s], ctx=cx + 1),
            remote(v_all.at[r], vp.at[r], fw_snd.at[1, s], fw_rcv.at[1, s], ctx=cx + 1),
        )

    def prefix_copy(off):
        dst = lax.rem(cx + off, n_ctx)
        r = part_rows(cx)
        return (
            remote(pk_ref, pk_all.at[r], pg_snd.at[0, dst], pg_rcv.at[0, cx], ctx=dst),
            remote(pv_ref, pv_all.at[r], pg_snd.at[1, dst], pg_rcv.at[1, cx], ctx=dst),
        )

    def back(kv):
        return remote(bk_send.at[kv], bk_recv.at[kv], bk_snd_sem.at[kv], bk_rcv_sem.at[kv], ctx=cx - 1)

    def reduce_copy(kv, off):
        dst = lax.rem(cx + off, n_ctx)
        return remote(psend.at[kv, dst], precv.at[kv, cx], pr_snd.at[kv, dst], pr_rcv.at[kv, cx], ctx=dst)

    def delta_copy(off):
        dst = peer(off)
        return remote(dl_send.at[dst], dl_recv.at[me], dl_snd_sem.at[dst], dl_rcv_sem.at[me], head=dst)

    def over_ctx(body):
        def step(off, carry):
            body(off)
            return carry
        lax.fori_loop(1, n_ctx, step, 0)

    barrier = pltpu.get_barrier_semaphore()
    for off in range(1, n_head):
        pl.semaphore_signal(barrier, inc=1, device_id={"head": peer(off)}, device_id_type=MESH)
    over_ctx(lambda off: pl.semaphore_signal(
        barrier, inc=1, device_id={"ctx": lax.rem(cx + off, n_ctx)}, device_id_type=MESH))

    get_g = pltpu.make_async_copy(g_hbm, g_vm, loc.at[0])
    get_o = pltpu.make_async_copy(o_hbm, o_vm, loc.at[1])
    get_g.start()
    get_o.start()
    small = (
        pltpu.make_async_copy(norm_hbm, norm_ref, loc.at[4]),
        pltpu.make_async_copy(blocks_hbm, blocks_ref, loc.at[5]),
        pltpu.make_async_copy(members_hbm, members_ref, loc.at[6]),
        pltpu.make_async_copy(pk_ref, pk_all.at[part_rows(cx)], loc.at[7]),
        pltpu.make_async_copy(pv_ref, pv_all.at[part_rows(cx)], loc.at[8]),
    )
    for c in small:
        c.start()
    own_kv = (
        pltpu.make_async_copy(k_hbm.at[:, kv_cols(me)], k_all.at[mine], loc.at[2]),
        pltpu.make_async_copy(v_hbm.at[:, kv_cols(me)], v_all.at[mine], loc.at[3]),
    )
    for c in own_kv:
        c.start()
    pl.semaphore_wait(barrier, n_head - 1 + n_ctx - 1)

    for off in (2, 1, 3):
        for c in kv_copy(off):
            c.start()
    for c in own_kv:
        c.wait()

    @pl.when(cx < n_ctx - 1)
    def _():
        for c in forward(me):
            c.start()

    def prefix_start(off):
        for c in prefix_copy(off):
            c.start()
    over_ctx(prefix_start)
    for h in range(EARLY):
        send_head(h)

    get_g.wait()
    get_o.wait()
    lane = lax.broadcasted_iota(jnp.int32, (rows, HD), 1)
    cols = jnp.zeros((rows, HD), F32)
    for d in range(n_head):
        for j in range(own):
            c = (d * own + j) * HD
            term = g_vm[:, c:c + HD].astype(F32) * o_vm[:, c:c + HD].astype(F32)
            total = jnp.sum(term, axis=1, keepdims=True)
            cols = jnp.where(lane == d * slot + j, total, cols)
    flipped = cols.T
    for d in range(n_head):
        dl_send[d] = flipped[d * slot:(d + 1) * slot]
    dl_recv[me] = dl_send[me]
    for off in (2, 1, 3):
        delta_copy(off).start()

    for off in (1, 3, 2):
        s = peer(off)
        arrived(k_all.at[from_rows(s)], kv_rcv.at[0, s])
        arrived(v_all.at[from_rows(s)], kv_rcv.at[1, s])

        @pl.when(cx < n_ctx - 1)
        def _():
            for c in forward(s):
                c.start()

    for h in range(EARLY, AHEAD):
        send_head(h)
    for c in small:
        c.wait()

    def scan(r, total):
        starts_s[r] = total
        return total + blocks_ref[r]
    lax.fori_loop(0, nresp, scan, jnp.int32(0))
    block = cx * (tokens // BLK) + lax.broadcasted_iota(jnp.int32, (1, tokens), 1) // BLK

    def place(i, carry):
        first, owner = carry
        p = i // members
        r = members_ref[p, lax.rem(i, members)]
        low = starts_s[r]
        inside = (block >= low) & (block < low + blocks_ref[r])
        return (jnp.where(inside, low * BLK, first), jnp.where(inside, p, owner))

    zero = jnp.zeros((1, tokens), jnp.int32)
    first, owner = lax.fori_loop(0, nprompt * members, place, (zero, zero))
    prompt_of[...] = owner
    first = first - cx * tokens
    key_at = lax.broadcasted_iota(jnp.int32, (tokens, tokens), 0)
    tok_at = lax.broadcasted_iota(jnp.int32, (tokens, tokens), 1)
    bias[0:tokens] = jnp.where(key_at - tokens >= first, 0.0, NEG)
    bias[tokens:2 * tokens] = jnp.where((key_at >= first) & (key_at <= tok_at), 0.0, NEG)

    def prefix_wait(off):
        s = lax.rem(cx + off, n_ctx)
        arrived(pk_all.at[part_rows(s)], pg_rcv.at[0, s])
        arrived(pv_all.at[part_rows(s)], pg_rcv.at[1, s])
    for off in (1, 3, 2):
        s = peer(off)
        arrived(dl_recv.at[s], dl_rcv_sem.at[s])

    dk_acc[...] = jnp.zeros_like(dk_acc)
    dv_acc[...] = jnp.zeros_like(dv_acc)
    pacc[...] = jnp.zeros_like(pacc)

    @pl.when(cx > 0)
    def _():
        dkp[...] = jnp.zeros_like(dkp)
        dvp[...] = jnp.zeros_like(dvp)

    def terms(keys, values, keys_t, qs, gs, norm, delta, mask):
        logits = lax.dot_general(keys, qs, NT, preferred_element_type=F32)
        weights = jnp.exp2(logits * (scale * LOG2E) + (mask - norm))
        weights_b = weights.astype(BF16)
        dv = jnp.dot(weights_b, gs, preferred_element_type=F32)
        dw = lax.dot_general(values, gs, NT, preferred_element_type=F32)
        dl = (weights * (dw - delta)).astype(BF16)
        dk = jnp.dot(dl, qs, preferred_element_type=F32)
        dq = jnp.dot(keys_t, dl, preferred_element_type=F32)
        return dq, dk, dv

    def of_head(h):
        norm = norm_ref[pl.ds(h, 1), :] * LOG2E
        delta = jnp.concatenate([dl_recv[s, pl.ds(h, 1), :] for s in range(n_head)], axis=1)
        return q_all[h], g_all[h], norm, delta

    kb = tokens // 2

    def add_dq(h, t, dq, first):
        if first:
            dq_acc[h, :, t] = dq
        else:
            dq_acc[h, :, t] += dq

    def here(kv, h, first):
        kc = slice(kv * HD, (kv + 1) * HD)
        qs, gs, norm, delta = of_head(h)
        for b in range(2):
            a, e = b * kb, (b + 1) * kb
            t = slice(a, tokens)
            dq, dk, dv = terms(
                k_all[a:e, kc], v_all[a:e, kc], kt[:, ptot + tokens + a:ptot + tokens + e],
                qs[t], gs[t], norm[:, t], delta[:, t], bias[tokens + a:tokens + e, t])
            dk_acc[kv, a:e] += dk
            dv_acc[kv, a:e] += dv
            add_dq(h, t, dq, first and b == 0)

    def elsewhere(kv, h, first):
        kc = slice(kv * HD, (kv + 1) * HD)
        every = slice(0, tokens)

        def prompt(p, sets):
            qs, gs, norm, delta = of_head(h)
            r = pl.ds(pl.multiple_of(p * PL, PL), PL)
            if nprompt == 1:
                mask = 0.0
            else:
                mask = jnp.where(prompt_of[...] == p, 0.0, NEG)
            dq, dk, dv = terms(pk_all[r, kc], pv_all[r, kc], kt[:, r], qs, gs, norm, delta, mask)
            c = pl.ds(p * (PL // part), PL // part)
            pacc[kv, c, 0] += dk.reshape(PL // part, part, HD)
            pacc[kv, c, 1] += dv.reshape(PL // part, part, HD)
            add_dq(h, every, dq, sets)

        prompt(0, first)
        if nprompt > 1:
            def more(p, carry):
                prompt(p, False)
                return carry
            lax.fori_loop(1, nprompt, more, 0)

        @pl.when(cx > 0)
        def _():
            qs, gs, norm, delta = of_head(h)
            for b in range(2):
                a, e = b * kb, (b + 1) * kb
                dq, dk, dv = terms(
                    kp[a:e, kc], vp[a:e, kc], kt[:, ptot + a:ptot + e],
                    qs, gs, norm, delta, bias[a:e])
                dkp[kv, a:e] += dk
                dvp[kv, a:e] += dv
                add_dq(h, every, dq, False)

    def give_back(kv):
        @pl.when(cx > 0)
        def _():
            bk_send[kv, 0] = dkp[kv].astype(BF16)
            bk_send[kv, 1] = dvp[kv].astype(BF16)
            back(kv).start()
        psend[kv] = pacc[kv].astype(BF16)
        over_ctx(lambda off: reduce_copy(kv, off).start())

    def write_dq(h):
        dq_out[h] = (dq_acc[h] * scale).T.astype(BF16)
        pltpu.make_async_copy(
            dq_out.at[h], dq_hbm.at[:, pl.ds(pl.multiple_of(h * HD, HD), HD)], dq_sem.at[h]
        ).start()

    def take_head(h):
        @pl.when(h + AHEAD < own)
        def _():
            send_head(h + AHEAD)
        for off in (0, 1, 3, 2):
            s = peer(off)
            arrived(q_all.at[h, from_rows(s)], q_rcv.at[h, s])
            arrived(g_all.at[h, from_rows(s)], g_rcv.at[h, s])

    def keys_from_elsewhere(kv):
        kc = slice(kv * HD, (kv + 1) * HD)
        if kv == 0:
            over_ctx(prefix_wait)
        kt[:, 0:ptot] = pk_all[:, kc].T

        @pl.when(cx > 0)
        def _():
            if kv == 0:
                for s in range(n_head):
                    arrived(kp.at[s * rows:(s + 1) * rows], fw_rcv.at[0, s])
                    arrived(vp.at[s * rows:(s + 1) * rows], fw_rcv.at[1, s])
            kt[:, ptot:ptot + tokens] = kp[:, kc].T

    for kv in range(kvl):
        kt[:, ptot + tokens:ptot + 2 * tokens] = k_all[:, kv * HD:(kv + 1) * HD].T
        if kv > 0:
            keys_from_elsewhere(kv)

        def step(i, carry):
            h = kv * grp + i

            @pl.when(i < grp)
            def _():
                take_head(h)
                if kv == 0:
                    here(kv, h, True)
                else:
                    elsewhere(kv, h, True)

            if kv == 0:
                @pl.when(i == LAG)
                def _():
                    keys_from_elsewhere(kv)
            else:
                @pl.when(i == grp - 1)
                def _():
                    give_back(kv)

            @pl.when(i >= LAG)
            def _():
                if kv == 0:
                    elsewhere(kv, h - LAG, False)
                else:
                    here(kv, h - LAG, False)
                write_dq(h - LAG)
            return carry

        lax.fori_loop(0, grp + LAG, step, 0)
        if kv == 0:
            give_back(kv)

    for kv in range(kvl):
        kc = slice(kv * HD, (kv + 1) * HD)

        def sum_wait(off):
            s = lax.rem(cx + off, n_ctx)
            arrived(precv.at[kv, s], pr_rcv.at[kv, s])
        over_ctx(sum_wait)
        total = lax.fori_loop(
            1, n_ctx, lambda off, t: t + precv[kv, lax.rem(cx + off, n_ctx)].astype(F32), pacc[kv, cx])
        dpk_ref[:, kc] = (total[0] * scale).astype(BF16)
        dpv_ref[:, kc] = total[1].astype(BF16)

        @pl.when(cx < n_ctx - 1)
        def _():
            arrived(bk_recv.at[kv], bk_rcv_sem.at[kv])
            dk_ref[:, kc] = ((dk_acc[kv] + bk_recv[kv, 0].astype(F32)) * scale).astype(BF16)
            dv_ref[:, kc] = (dv_acc[kv] + bk_recv[kv, 1].astype(F32)).astype(BF16)

        @pl.when(cx == n_ctx - 1)
        def _():
            dk_ref[:, kc] = (dk_acc[kv] * scale).astype(BF16)
            dv_ref[:, kc] = dv_acc[kv].astype(BF16)

    def finish(h, carry):
        pltpu.make_async_copy(
            dq_out.at[h], dq_hbm.at[:, pl.ds(pl.multiple_of(h * HD, HD), HD)], dq_sem.at[h]
        ).wait()
        for off in (2, 1, 3):
            for c in q_copy(h, off):
                c.wait_send()
        return carry
    lax.fori_loop(0, own, finish, 0)
    for off in (2, 1, 3):
        for c in kv_copy(off):
            c.wait_send()
        delta_copy(off).wait_send()

    @pl.when(cx < n_ctx - 1)
    def _():
        for s in range(n_head):
            for c in forward(s):
                c.wait_send()

    @pl.when(cx > 0)
    def _():
        for kv in range(kvl):
            back(kv).wait_send()

    def sent(off):
        for c in prefix_copy(off):
            c.wait_send()
        for kv in range(kvl):
            reduce_copy(kv, off).wait_send()
    over_ctx(sent)


def place_results(*refs):
    count = (len(refs) - 2) // 3
    ins, outs, held, (got, put) = refs[:count], refs[count:2 * count], refs[2 * count:-2], refs[-2:]
    steps = []
    for i in range(count):
        pieces = PIECES if i == 0 else 1
        rows = ins[i].shape[0] // pieces
        for p in range(pieces):
            at = pl.ds(p * rows, rows)
            n = len(steps)
            steps.append((
                pltpu.make_async_copy(ins[i].at[at], held[i].at[at], got.at[n]),
                pltpu.make_async_copy(held[i].at[at], outs[i].at[at], put.at[n]),
            ))
    for get, _ in steps:
        get.start()
    for get, send in steps:
        get.wait()
        send.start()
    for _, send in steps:
        send.wait()


def shards(n_ctx, n_head, *arrays):
    query_rows, key_rows, _, _, _, log_norm, prefix_keys, _, blocks, members = arrays
    rows, total_width = query_rows.shape
    own = log_norm.shape[0]
    kvw = prefix_keys.shape[1]
    kvl = kvw // HD
    tokens = rows * n_head
    nprompt = members.shape[0]
    ptot = nprompt * PL
    part = prefix_keys.shape[0]
    slot = -(-own // 8) * 8
    hbm = pl.BlockSpec(memory_space=pl.ANY)
    vmem = pl.BlockSpec(memory_space=pltpu.VMEM)
    dma = pltpu.SemaphoreType.DMA
    results = pl.pallas_call(
        functools.partial(
            kernel, n_ctx=n_ctx, n_head=n_head, nprompt=nprompt, own=own, kvl=kvl),
        out_shape=(
            jax.ShapeDtypeStruct((tokens, own * HD), BF16),
            jax.ShapeDtypeStruct((tokens, kvw), BF16),
            jax.ShapeDtypeStruct((tokens, kvw), BF16),
            jax.ShapeDtypeStruct((part, kvw), BF16),
            jax.ShapeDtypeStruct((part, kvw), BF16),
        ),
        in_specs=[hbm] * 10,
        out_specs=(hbm, vmem, vmem, vmem, vmem),
        scratch_shapes=[
            pltpu.VMEM((own, tokens, HD), BF16),
            pltpu.VMEM((own, tokens, HD), BF16),
            pltpu.VMEM((tokens, kvw), BF16),
            pltpu.VMEM((tokens, kvw), BF16),
            pltpu.VMEM((tokens, kvw), BF16),
            pltpu.VMEM((tokens, kvw), BF16),
            pltpu.VMEM((ptot, kvw), BF16),
            pltpu.VMEM((ptot, kvw), BF16),
            pltpu.VMEM((HD, ptot + 2 * tokens), BF16),
            pltpu.VMEM((rows, total_width), BF16),
            pltpu.VMEM((rows, total_width), BF16),
            pltpu.VMEM(log_norm.shape, F32),
            pltpu.SMEM(blocks.shape, jnp.int32),
            pltpu.SMEM(members.shape, jnp.int32),
            pltpu.VMEM((n_head, slot, rows), F32),
            pltpu.VMEM((n_head, slot, rows), F32),
            pltpu.VMEM((2 * tokens, tokens), F32),
            pltpu.VMEM((1, tokens), jnp.int32),
            pltpu.SMEM(blocks.shape, jnp.int32),
            pltpu.VMEM((own, HD, tokens), F32),
            pltpu.VMEM((own, tokens, HD), BF16),
            pltpu.VMEM((kvl, tokens, HD), F32),
            pltpu.VMEM((kvl, tokens, HD), F32),
            pltpu.VMEM((kvl, tokens, HD), F32),
            pltpu.VMEM((kvl, tokens, HD), F32),
            pltpu.VMEM((kvl, 2, tokens, HD), BF16),
            pltpu.VMEM((kvl, 2, tokens, HD), BF16),
            pltpu.VMEM((kvl, n_ctx, 2, part, HD), F32),
            pltpu.VMEM((kvl, n_ctx, 2, part, HD), BF16),
            pltpu.VMEM((kvl, n_ctx, 2, part, HD), BF16),
            dma((own, n_head)), dma((own, n_head)), dma((own, n_head)), dma((own, n_head)),
            dma((2, n_head)), dma((2, n_head)), dma((2, n_head)), dma((2, n_head)),
            dma((2, n_ctx)), dma((2, n_ctx)),
            dma((kvl, n_ctx)), dma((kvl, n_ctx)),
            dma((kvl,)), dma((kvl,)),
            dma((n_head,)), dma((n_head,)),
            dma((9,)), dma((own,)),
        ],
        compiler_params=pltpu.CompilerParams(
            collective_id=0, has_side_effects=True, vmem_limit_bytes=VMEM_BYTES),
    )(*arrays)
    return pl.pallas_call(
        place_results,
        out_shape=tuple(jax.ShapeDtypeStruct(a.shape, a.dtype) for a in results),
        in_specs=[hbm] * len(results),
        out_specs=(hbm,) * len(results),
        scratch_shapes=[pltpu.VMEM(a.shape, a.dtype) for a in results]
        + [dma((len(results) + PIECES,))] * 2,
    )(*results)


def solution(mesh):
    placed = (
        P(("ctx", "head"), None),
        P(("ctx", "head"), None),
        P(("ctx", "head"), None),
        P(("ctx", "head"), None),
        P(("ctx", "head"), None),
        P("head", "ctx"),
        P("ctx", "head"),
        P("ctx", "head"),
        P(),
        P(),
    )
    return jax.shard_map(
        functools.partial(shards, mesh.shape["ctx"], mesh.shape["head"]),
        mesh=mesh,
        in_specs=placed,
        out_specs=(
            P("ctx", "head"),
            P("ctx", "head"),
            P("ctx", "head"),
            P("ctx", "head"),
            P("ctx", "head"),
        ),
        check_vma=False,
    )
```
